256 devices in a mesh: seq: 32 (over y, x, core), head: 8 (over z).
Axes of the slice: x: 4, y: 4, z: 8, core: 2. Of those that a mesh axis runs over, the one named last changes fastest.
Arguments:
- queries: bfloat16 [65536, 8192], P(('seq', 'head')), may hold values from -8 to 8
- keys: bfloat16 [65536, 1024], P(('seq', 'head')), may hold values from -8 to 8
- values: bfloat16 [65536, 1024], P(('seq', 'head')), may hold values from -6 to 6
- doc_block: int32 [512], replicated, may hold values from 0 to 511, as said below
- balance: int32 [512], replicated, may hold values from 0 to 511, as said below
Outputs:
- attended: bfloat16 [65536, 8192], P(('seq', 'head'))
The draws below stay inside these ranges and needn't reach their ends.
Inputs may be any that keep to these rules, and one draw needn't show every extreme that they name: `balance`: each value once. Seq group g takes positions g * 16 to (g + 1) * 16 - 1; no two blocks that start in the same seq group (same b // 16) are placed in the same seq group, and every seq group receives blocks from 16 different source groups. `doc_block`: the blocks of one document take consecutive positions of balance inside one seq group, at most 4 of them; in every seq group one document has 4. A document's label is the largest index among its blocks.
All inputs are finite; a program needn't handle non-finite values.
Results may differ from the reference program's by a relative error of at most 0.0046.
Values may be sent and summed in bfloat16 or wider, within the bound.
A program may use at most 128 MiB of HBM per device.

```python
import math
import jax
import jax.numpy as jnp
from jax import lax

HEADS = 64
KV_HEADS = 8
HEAD_DIM = 128
BLOCK = 128
MOSTB = 4
TOKENS = 65536
GROUP_BLOCKS = 16


def block_layout(key):
    per_group = GROUP_BLOCKS
    group_count = TOKENS // (BLOCK * GROUP_BLOCKS)
    block_total = group_count * per_group
    sigma = jax.random.permutation(jax.random.fold_in(key, 11), group_count)
    shifts = jax.random.permutation(jax.random.fold_in(key, 12), group_count)
    slot_ids = jnp.arange(per_group, dtype=jnp.int32)
    sources = sigma[(shifts[:, None] + slot_ids[None, :]) % group_count]
    anchor = sources * per_group + slot_ids[None, :]
    row_keys = jax.random.split(jax.random.fold_in(key, 13), group_count)
    shuffled = jax.vmap(lambda row_key: jax.random.permutation(row_key, per_group))(row_keys)
    targets = jnp.arange(group_count, dtype=jnp.int32)[:, None] * per_group + shuffled
    order = jnp.zeros((block_total,), jnp.int32).at[targets.reshape(-1)].set(anchor.reshape(-1).astype(jnp.int32))
    coin_flips = jax.random.randint(jax.random.fold_in(key, 14), (group_count, per_group), 0, 2)

    def mark_group(coin_row):

        def advance(run_length, inputs_pair):
            slot_index, coin_flip = inputs_pair
            opening = (slot_index == 0) | (slot_index >= MOSTB) & ((coin_flip == 1) | (run_length >= MOSTB))
            run_length = jnp.where(opening, 1, run_length + 1)
            return (run_length, opening.astype(jnp.int32))
        final_run, openings = lax.scan(advance, jnp.int32(0), (slot_ids, coin_row))
        return openings
    openings = jax.vmap(mark_group)(coin_flips)
    doc_index = jnp.cumsum(openings.reshape(-1)) - 1
    same_doc = doc_index[:, None] == doc_index[None, :]
    label = jnp.max(jnp.where(same_doc, order[None, :], -1), axis=1)
    labels = jnp.zeros((block_total,), jnp.int32).at[order].set(label.astype(jnp.int32))
    return (order, labels)


def draw_balance(key, part):
    order, labels = block_layout(key)
    return order


def draw_doc_block(key, part):
    order, labels = block_layout(key)
    return labels


def draw_queries(key, part):
    key = jax.random.fold_in(key, 23)
    base = jnp.clip(jax.random.normal(key, (TOKENS, HEADS, HEAD_DIM), jnp.float32), -8.0, 8.0)
    return base.reshape(TOKENS, HEADS * HEAD_DIM).astype(jnp.bfloat16)


def draw_keys(key, part):
    key = jax.random.fold_in(key, 24)
    base = jnp.clip(jax.random.normal(key, (TOKENS, KV_HEADS, HEAD_DIM), jnp.float32), -8.0, 8.0)
    return base.reshape(TOKENS, KV_HEADS * HEAD_DIM).astype(jnp.bfloat16)


def shard_levels(own_key, shape, cuts, low, top_value):
    level, own = 1.0, jax.random.fold_in(own_key, 6)
    for position, shards_of in cuts:
        heights = jnp.exp(jax.random.uniform(jax.random.fold_in(own, position), (shards_of,), jnp.float32, low / len(cuts), top_value / len(cuts)))
        level = level * jnp.repeat(heights, shape[position] // shards_of).reshape([-1 if axis == position else 1 for axis in range(len(shape))])
    return level


def bell_draw(rng, dims, deviation, limit, pieces=(), kind=jnp.bfloat16):
    values = jax.random.normal(rng, dims, jnp.float32) * deviation
    if len(pieces) > 0:
        values = shard_levels(rng, dims, pieces, -0.22, 0.18) * values
    return jnp.clip(values, min=-limit, max=limit).astype(kind)


def setup_inputs(seed: int = 0) -> dict:
    arg_keys = jax.random.split(jax.random.key(seed), 6)
    return {
        "queries": draw_queries(jax.random.fold_in(arg_keys[5], 71), 0),
        "keys": draw_keys(jax.random.fold_in(arg_keys[5], 71), 0),
        "values": bell_draw(arg_keys[2], (TOKENS, KV_HEADS * HEAD_DIM), 1.0, 6.0, ((0, 256),)),
        "doc_block": draw_doc_block(jax.random.fold_in(arg_keys[5], 71), 0),
        "balance": draw_balance(jax.random.fold_in(arg_keys[5], 71), 0),
    }


def attend_block(query_blk, key_win, value_win, query_rank, query_doc, key_rank, key_doc):
    kv_count = key_win.shape[1]
    grouped = query_blk.reshape(BLOCK, kv_count, -1, HEAD_DIM).astype(jnp.float32)
    scores = jnp.einsum('tkgd,ukd->kgtu', grouped, key_win.astype(jnp.float32)) * (1.0 / math.sqrt(HEAD_DIM))
    allowed = (key_doc[None, :] == query_doc) & (key_rank[None, :] <= query_rank[:, None])
    scores = jnp.where(allowed[None, None, :, :], scores, -jnp.inf)
    top_score = lax.optimization_barrier(jnp.max(scores, axis=-1, keepdims=True))
    raised = jnp.exp(scores - top_score)
    weights = (raised / lax.optimization_barrier(jnp.sum(raised, axis=-1, keepdims=True))).astype(jnp.bfloat16)
    mixed = jnp.einsum('kgtu,ukd->tkgd', weights.astype(jnp.float32), value_win.astype(jnp.float32))
    return mixed.reshape(BLOCK, -1).astype(jnp.bfloat16)

def reference(queries, keys, values, doc_block, balance):
    block_total = TOKENS // BLOCK
    width = min(MOSTB, GROUP_BLOCKS)
    positions = jnp.arange(block_total, dtype=jnp.int32)
    inverse = jnp.zeros((block_total,), jnp.int32).at[balance].set(positions)
    group_start = positions // GROUP_BLOCKS * GROUP_BLOCKS
    first_pos = group_start + jnp.clip(positions % GROUP_BLOCKS - width + 1, 0, GROUP_BLOCKS - width)
    win_pos = first_pos[:, None] + jnp.arange(width, dtype=jnp.int32)[None, :]
    offsets = jnp.arange(BLOCK, dtype=jnp.int32)
    query_blocks = queries.reshape(block_total, BLOCK, HEADS * HEAD_DIM)
    key_blocks = keys.reshape(block_total, BLOCK, KV_HEADS, HEAD_DIM)
    value_blocks = values.reshape(block_total, BLOCK, KV_HEADS, HEAD_DIM)

    def per_block(block_id):
        place = inverse[block_id]
        window = win_pos[place]
        sources = balance[window]
        key_win = key_blocks[sources].reshape(width * BLOCK, KV_HEADS, HEAD_DIM)
        value_win = value_blocks[sources].reshape(width * BLOCK, KV_HEADS, HEAD_DIM)
        key_rank = (window[:, None] * BLOCK + offsets[None, :]).reshape(width * BLOCK)
        key_doc = jnp.broadcast_to(doc_block[sources][:, None], (width, BLOCK)).reshape(width * BLOCK)
        query_rank = place * BLOCK + offsets
        return attend_block(query_blocks[block_id], key_win, value_win, query_rank, doc_block[block_id], key_rank, key_doc)
    mixed = lax.map(per_block, positions)
    return mixed.reshape(TOKENS, HEADS * HEAD_DIM)
```

```python
import functools
import math

import jax
import jax.numpy as jnp
from jax import lax
from jax.experimental import pallas as pl
from jax.experimental.pallas import tpu as pltpu
from jax.sharding import PartitionSpec as P

HEAD_DIM = 128
BLOCK = 128
BLOCKS = 512
GROUP = 16
KV = 8
SEQ = 32
ZS = 8
ITEMS = 64
WINDOW = 3
NEED = 2 * WINDOW
CHUNKS = 4
FAST = 16
SLOW = 64
MESH = pl.DeviceIdType.MESH
SCALE = math.log2(math.e) / math.sqrt(HEAD_DIM)


def table_kernel(balance_ref, doc_ref, table_ref):
    seq = lax.axis_index("seq")
    z = lax.axis_index("head")
    f32 = jnp.float32
    balance = balance_ref[...]
    doc = doc_ref[...].astype(f32)
    rows = lax.broadcasted_iota(jnp.int32, (BLOCKS, BLOCKS), 0)
    cols = lax.broadcasted_iota(jnp.int32, (BLOCKS, BLOCKS), 1)
    doc_col = jnp.sum(jnp.where(rows == cols, doc, 0.0), axis=1, keepdims=True)
    label = jnp.sum(jnp.where(rows == balance, doc_col, 0.0), axis=0, keepdims=True)
    position = lax.broadcasted_iota(jnp.int32, (1, BLOCKS), 1)
    z_of = balance % GROUP // 2
    item = balance // GROUP * 2 + balance % 2
    zs = lax.broadcasted_iota(jnp.int32, (ZS, BLOCKS), 0)
    uses = (zs == z_of).astype(f32)
    wanted = jnp.zeros((ZS, BLOCKS), f32)
    valid = []
    for w in range(1, WINDOW + 1):
        same = (position % GROUP >= w) & (pltpu.roll(label, w, 1) == label)
        same = same.astype(f32)
        valid.append(same)
        wanted = jnp.maximum(wanted, pltpu.roll(uses * same, BLOCKS - w, 1))
    to_mine = jnp.sum(jnp.where(zs == z, wanted, 0.0), axis=0, keepdims=True)
    sends = jnp.where(z_of == z, wanted, 0.0)
    receives = uses * to_mine
    members = jnp.concatenate([sends, receives], axis=0)
    before = (rows < cols).astype(f32).astype(jnp.bfloat16)
    ranks = jnp.dot(members.astype(jnp.bfloat16), before, preferred_element_type=f32)
    counts = jnp.zeros((ZS, 1), f32)
    for other in range(ZS):
        count = jnp.sum(uses * wanted[other : other + 1, :], axis=1, keepdims=True)
        own = lax.broadcasted_iota(jnp.int32, (ZS, 1), 0) == other
        counts = jnp.maximum(counts, jnp.where(own, 0.0, count))
    most = jnp.max(counts, axis=0, keepdims=True)
    rank_in = jnp.sum(receives * ranks[ZS:, :], axis=0, keepdims=True)
    z_float = z_of.astype(f32)
    item_float = item.astype(f32)
    lanes = lax.broadcasted_iota(jnp.int32, (ITEMS, 128), 1)
    table = jnp.where(lanes == 14, most, 0.0)
    slot = lax.broadcasted_iota(jnp.int32, (ITEMS, BLOCKS), 0).astype(f32)
    for other in range(ZS):
        rank = jnp.where(members[other : other + 1, :] > 0.0, ranks[other : other + 1, :], -1.0)
        picked = jnp.sum(jnp.where(slot == rank, item_float, 0.0), axis=1, keepdims=True)
        table = jnp.where(lanes == other, picked, table)
    row64 = lax.broadcasted_iota(jnp.int32, (ITEMS, BLOCKS), 0)
    consumer = row64 // 2 * GROUP + z * 2 + row64 % 2
    match = consumer == balance
    for fast, lane in ((FAST, 8), (SLOW, 11)):
        place = jnp.where(z_of == z, item_float, ITEMS + z_float * fast + rank_in)
        for w in range(1, WINDOW + 1):
            source = pltpu.roll(place, w, 1) * valid[w - 1]
            found = jnp.sum(jnp.where(match, source, 0.0), axis=1, keepdims=True)
            table = jnp.where(lanes == lane + w - 1, found, table)
    in_use = valid[0] + valid[0] * valid[1] + valid[0] * valid[1] * valid[2]
    for t in range(2):
        mine = balance == seq * GROUP + z * 2 + t
        used = jnp.sum(jnp.where(mine, in_use, 0.0), axis=1, keepdims=True)
        table = jnp.where(lanes == 15 + t, used, table)
    table_ref[...] = table.astype(jnp.int32)


def make_table(balance, doc_block):
    return pl.pallas_call(
        table_kernel,
        out_shape=jax.ShapeDtypeStruct((ITEMS, 128), jnp.int32),
        in_specs=[pl.BlockSpec(memory_space=pltpu.VMEM)] * 2,
        out_specs=pl.BlockSpec(memory_space=pltpu.VMEM),
        name="table",
    )(balance.reshape(1, BLOCKS), doc_block.reshape(1, BLOCKS))


def exchange_kernel(cap, table_ref, key_ref, value_ref, out_ref, *scratch):
    pieces, landed, held, packed, final, sends, arrivals, local = scratch_lists(scratch)
    seq = lax.axis_index("seq")
    z = lax.axis_index("head")
    place_lane = 8 if cap == FAST else 11

    def plane_peer(step):
        step = step * 13 % SEQ
        y = (seq // 8 + step // 8) % 4
        x = (seq // 2 + step // 2) % 4
        core = (seq + step) % 2
        return y * 8 + x * 2 + core

    barrier = pltpu.get_barrier_semaphore()

    def greet_plane(step, carry):
        pl.semaphore_signal(barrier, inc=1, device_id=(plane_peer(step), z), device_id_type=MESH)
        return carry

    def greet_z(step, carry):
        pl.semaphore_signal(barrier, inc=1, device_id=(seq, (z + step) % ZS), device_id_type=MESH)
        return carry

    lax.fori_loop(1, SEQ, greet_plane, 0)
    lax.fori_loop(1, ZS, greet_z, 0)

    for chunk in range(CHUNKS):
        source = key_ref if chunk < 2 else value_ref
        for head in range(KV):
            for quarter in range(4):
                for t in range(2):
                    row = t * BLOCK + quarter * 32 + chunk % 2 * 16
                    pieces[chunk][head * 4 + quarter, t] = source[
                        row : row + 16, head * HEAD_DIM : (head + 1) * HEAD_DIM
                    ]
    pl.semaphore_wait(barrier, SEQ - 1 + ZS - 1)

    def spread(chunk):
        def send(step, carry):
            peer = plane_peer(step)
            pltpu.make_async_remote_copy(
                src_ref=pieces[chunk].at[peer],
                dst_ref=landed[chunk].at[seq],
                send_sem=sends.at[0, chunk],
                recv_sem=arrivals.at[0, chunk],
                device_id=(peer, z),
                device_id_type=MESH,
            ).start()
            return carry

        lax.fori_loop(1, SEQ, send, 0)
        landed[chunk][seq] = pieces[chunk][seq]

    def across(chunk):
        whole = landed[chunk].at[pl.ds(0, SEQ - 1)]
        pltpu.make_async_copy(whole, whole, arrivals.at[0, chunk]).wait()

        def pack(step, carry):
            other = (z + step) % ZS
            for k in range(cap):
                index = table_ref[k, other]
                packed[chunk][other, k] = landed[chunk][index // 2, index % 2]
            pltpu.make_async_remote_copy(
                src_ref=packed[chunk].at[other],
                dst_ref=held[chunk].at[pl.ds(ITEMS + z * cap, cap)],
                send_sem=sends.at[1, chunk],
                recv_sem=arrivals.at[1, chunk],
                device_id=(seq, other),
                device_id_type=MESH,
            ).start()
            return carry

        lax.fori_loop(1, ZS, pack, 0)

        def keep(k, carry):
            held[chunk][2 * k] = landed[chunk][k, 0]
            held[chunk][2 * k + 1] = landed[chunk][k, 1]
            return carry

        lax.fori_loop(0, SEQ, keep, 0)

        def blank(k, carry):
            held[chunk][ITEMS + z * cap + k] = jnp.zeros((16, HEAD_DIM), jnp.bfloat16)
            return carry

        lax.fori_loop(0, cap, blank, 0)

    def deliver(chunk):
        whole = held[chunk].at[pl.ds(0, (ZS - 1) * cap)]
        pltpu.make_async_copy(whole, whole, arrivals.at[1, chunk]).wait()

        def fill(peer):
            for n in range(NEED):
                index = table_ref[peer * 2 + n // WINDOW, place_lane + n % WINDOW]
                final[chunk][peer, n] = held[chunk][index]

        def pack(step, carry):
            peer = plane_peer(step)
            fill(peer)
            pltpu.make_async_remote_copy(
                src_ref=final[chunk].at[peer],
                dst_ref=out_ref.at[chunk, seq],
                send_sem=sends.at[2, chunk],
                recv_sem=arrivals.at[2, chunk],
                device_id=(peer, z),
                device_id_type=MESH,
            ).start()
            return carry

        lax.fori_loop(1, SEQ, pack, 0)
        fill(seq)
        pltpu.make_async_copy(final[chunk].at[seq], out_ref.at[chunk, seq], local.at[chunk]).start()

    for chunk in range(CHUNKS):
        spread(chunk)
    for chunk in range(CHUNKS):
        across(chunk)
    for chunk in range(CHUNKS):
        deliver(chunk)
    for chunk in range(CHUNKS):
        pltpu.make_async_copy(final[chunk].at[seq], out_ref.at[chunk, seq], local.at[chunk]).wait()
        whole = out_ref.at[chunk, pl.ds(0, SEQ - 1)]
        pltpu.make_async_copy(whole, whole, arrivals.at[2, chunk]).wait()
        gone = pieces[chunk].at[pl.ds(0, SEQ - 1)]
        pltpu.make_async_copy(gone, gone, sends.at[0, chunk]).wait()
        gone = packed[chunk].at[pl.ds(0, ZS - 1)]
        pltpu.make_async_copy(gone, gone, sends.at[1, chunk]).wait()
        gone = final[chunk].at[pl.ds(0, SEQ - 1)]
        pltpu.make_async_copy(gone, gone, sends.at[2, chunk]).wait()


def scratch_lists(scratch):
    lists = [scratch[k * CHUNKS : (k + 1) * CHUNKS] for k in range(5)]
    return (*lists, *scratch[5 * CHUNKS :])


def exchange(cap, ident, table, keys, values):
    tile = (16, HEAD_DIM)
    shapes = ((SEQ, 2), (SEQ, 2), (ITEMS + ZS * cap,), (ZS, cap), (SEQ, NEED))
    buffers = [pltpu.VMEM(s + tile, jnp.bfloat16) for s in shapes for _ in range(CHUNKS)]
    return pl.pallas_call(
        functools.partial(exchange_kernel, cap),
        out_shape=jax.ShapeDtypeStruct((CHUNKS, SEQ, NEED) + tile, jnp.bfloat16),
        in_specs=[
            pl.BlockSpec(memory_space=pltpu.SMEM),
            pl.BlockSpec(memory_space=pltpu.VMEM),
            pl.BlockSpec(memory_space=pltpu.VMEM),
        ],
        out_specs=pl.BlockSpec(memory_space=pl.ANY),
        scratch_shapes=buffers
        + [
            pltpu.SemaphoreType.DMA((3, CHUNKS)),
            pltpu.SemaphoreType.DMA((3, CHUNKS)),
            pltpu.SemaphoreType.DMA((CHUNKS,)),
        ],
        compiler_params=pltpu.CompilerParams(
            collective_id=ident, has_side_effects=True, vmem_limit_bytes=48 * 1024 * 1024
        ),
        name=f"exchange_{cap}",
    )(table, keys, values)


def attend_kernel(used_ref, query_ref, key_ref, value_ref, window_ref, out_ref):
    group = query_ref.shape[1] // HEAD_DIM
    ones = jnp.ones((BLOCK, HEAD_DIM), jnp.bfloat16)
    above = lax.broadcasted_iota(jnp.int32, (BLOCK, BLOCK), 1) > lax.broadcasted_iota(
        jnp.int32, (BLOCK, BLOCK), 0
    )

    def block(t, windows):
        rows = slice(t * BLOCK, (t + 1) * BLOCK)
        keys = [key_ref[rows, :]]
        values = [value_ref[rows, :]]
        for w in range(windows):
            n = t * WINDOW + w
            keys.append(window_ref[0:2, :, n].reshape(BLOCK, HEAD_DIM))
            values.append(window_ref[2:4, :, n].reshape(BLOCK, HEAD_DIM))
        keys = jnp.concatenate(keys, axis=0)
        values = jnp.concatenate(
            [jnp.concatenate([v, ones], axis=1) for v in values], axis=0
        )
        query = jnp.concatenate(
            [query_ref[rows, h * HEAD_DIM : (h + 1) * HEAD_DIM] for h in range(group)], axis=0
        )
        scores = lax.dot_general(
            query, keys, (((1,), (1,)), ((), ())), preferred_element_type=jnp.float32
        )
        own = scores[:, :BLOCK].reshape(group, BLOCK, BLOCK)
        own = jnp.where(above[None], -jnp.inf, own).reshape(group * BLOCK, BLOCK)
        scores = jnp.concatenate([own, scores[:, BLOCK:]], axis=1) if windows else own
        top = jnp.max(scores, axis=1, keepdims=True)
        weights = jnp.exp2((scores - top) * SCALE).astype(jnp.bfloat16)
        mixed = jnp.dot(weights, values, preferred_element_type=jnp.float32)
        result = (mixed[:, :HEAD_DIM] / mixed[:, HEAD_DIM:]).astype(jnp.bfloat16)
        for h in range(group):
            out_ref[rows, h * HEAD_DIM : (h + 1) * HEAD_DIM] = result[
                h * BLOCK : (h + 1) * BLOCK, :
            ]

    for t in range(2):
        for windows in range(WINDOW + 1):
            pl.when(used_ref[t] == windows)(functools.partial(block, t, windows))


def attend(used, queries, keys, values, window):
    tokens, width = queries.shape
    columns = width // KV
    spec = pltpu.PrefetchScalarGridSpec(
        num_scalar_prefetch=1,
        grid=(KV,),
        in_specs=[
            pl.BlockSpec((tokens, columns), lambda k, used: (0, k)),
            pl.BlockSpec((tokens, HEAD_DIM), lambda k, used: (0, k)),
            pl.BlockSpec((tokens, HEAD_DIM), lambda k, used: (0, k)),
            pl.BlockSpec((CHUNKS, 4, NEED, 16, HEAD_DIM), lambda k, used: (0, k, 0, 0, 0)),
        ],
        out_specs=pl.BlockSpec((tokens, columns), lambda k, used: (0, k)),
    )
    return pl.pallas_call(
        attend_kernel,
        out_shape=jax.ShapeDtypeStruct(queries.shape, queries.dtype),
        grid_spec=spec,
        compiler_params=pltpu.CompilerParams(vmem_limit_bytes=48 * 1024 * 1024),
        name="attend",
    )(used, queries, keys, values, window)


def shards(queries, keys, values, doc_block, balance):
    table = make_table(balance, doc_block)
    window = lax.cond(
        table[0, 14] <= FAST,
        functools.partial(exchange, FAST, 0),
        functools.partial(exchange, SLOW, 1),
        table,
        keys,
        values,
    )
    return attend(table[0, 15:17], queries, keys, values, window)


def solution(mesh):
    in_specs = (
        P(("seq", "head"), None),
        P(("seq", "head"), None),
        P(("seq", "head"), None),
        P(),
        P(),
    )
    out_specs = P(("seq", "head"), None)
    return jax.shard_map(shards, mesh=mesh, in_specs=in_specs, out_specs=out_specs, check_vma=False)
```

```python
import functools
import math

import jax
import jax.numpy as jnp
from jax import lax
from jax.experimental import pallas as pl
from jax.experimental.pallas import tpu as pltpu
from jax.sharding import PartitionSpec as P

HEAD_DIM = 128
BLOCK = 128
BLOCKS = 512
GROUP = 16
KV = 8
SEQ = 32
ZS = 8
ITEMS = 64
WINDOW = 3
NEED = 2 * WINDOW
CHUNKS = 4
HEADS = KV // CHUNKS
TILES = BLOCK // 16
CAPS = (13, 16, 64)
MIB = 1024 * 1024
MESH = pl.DeviceIdType.MESH
SCALE = math.log2(math.e) / math.sqrt(HEAD_DIM)


def table_kernel(balance_ref, doc_ref, table_ref, branch_ref):
    seq = lax.axis_index("seq")
    z = lax.axis_index("head")
    f32 = jnp.float32
    balance = balance_ref[...]
    doc = doc_ref[...].astype(f32)
    rows = lax.broadcasted_iota(jnp.int32, (BLOCKS, BLOCKS), 0)
    cols = lax.broadcasted_iota(jnp.int32, (BLOCKS, BLOCKS), 1)
    doc_col = jnp.sum(jnp.where(rows == cols, doc, 0.0), axis=1, keepdims=True)
    label = jnp.sum(jnp.where(rows == balance, doc_col, 0.0), axis=0, keepdims=True)
    position = lax.broadcasted_iota(jnp.int32, (1, BLOCKS), 1)
    z_of = balance % GROUP // 2
    item = balance // GROUP * 2 + balance % 2
    zs = lax.broadcasted_iota(jnp.int32, (ZS, BLOCKS), 0)
    uses = (zs == z_of).astype(f32)
    wanted = jnp.zeros((ZS, BLOCKS), f32)
    valid = []
    for w in range(1, WINDOW + 1):
        same = (position % GROUP >= w) & (pltpu.roll(label, w, 1) == label)
        same = same.astype(f32)
        valid.append(same)
        wanted = jnp.maximum(wanted, pltpu.roll(uses * same, BLOCKS - w, 1))
    to_mine = jnp.sum(jnp.where(zs == z, wanted, 0.0), axis=0, keepdims=True)
    sends = jnp.where(z_of == z, wanted, 0.0)
    receives = uses * to_mine
    members = jnp.concatenate([sends, receives], axis=0)
    before = (rows < cols).astype(f32).astype(jnp.bfloat16)
    ranks = jnp.dot(members.astype(jnp.bfloat16), before, preferred_element_type=f32)
    counts = jnp.zeros((ZS, 1), f32)
    for other in range(ZS):
        count = jnp.sum(uses * wanted[other : other + 1, :], axis=1, keepdims=True)
        own = lax.broadcasted_iota(jnp.int32, (ZS, 1), 0) == other
        counts = jnp.maximum(counts, jnp.where(own, 0.0, count))
    most = jnp.max(counts)
    branch = jnp.int32(0)
    for cap in CAPS[:-1]:
        branch = branch + (most > cap).astype(jnp.int32)
    branch_ref[0] = branch
    rank_in = jnp.sum(receives * ranks[ZS:, :], axis=0, keepdims=True)
    item_float = item.astype(f32)
    lanes = lax.broadcasted_iota(jnp.int32, (ITEMS, 128), 1)
    table = jnp.zeros((ITEMS, 128), f32)
    slot = lax.broadcasted_iota(jnp.int32, (ITEMS, BLOCKS), 0)
    for other in range(ZS):
        rank = jnp.where(members[other : other + 1, :] > 0.0, ranks[other : other + 1, :], -1.0)
        picked = jnp.sum(
            jnp.where(slot.astype(f32) == rank, item_float, 0.0), axis=1, keepdims=True
        )
        table = jnp.where(lanes == other, picked, table)
    match = slot // 2 * GROUP + z * 2 + slot % 2 == balance
    place = jnp.where(z_of == z, item_float, ITEMS + rank_in)
    region = jnp.where(z_of == z, 0.0, z_of.astype(f32))
    for lane, what in ((8, place), (11, region)):
        for w in range(1, WINDOW + 1):
            source = pltpu.roll(what, w, 1) * valid[w - 1]
            found = jnp.sum(jnp.where(match, source, 0.0), axis=1, keepdims=True)
            table = jnp.where(lanes == lane + w - 1, found, table)
    in_use = valid[0] + valid[0] * valid[1] + valid[0] * valid[1] * valid[2]
    for t in range(2):
        mine = balance == seq * GROUP + z * 2 + t
        used = jnp.sum(jnp.where(mine, in_use, 0.0), axis=1, keepdims=True)
        table = jnp.where(lanes == 15 + t, used, table)
    table_ref[...] = table.astype(jnp.int32)


def make_table(balance, doc_block):
    return pl.pallas_call(
        table_kernel,
        out_shape=(
            jax.ShapeDtypeStruct((ITEMS, 128), jnp.int32),
            jax.ShapeDtypeStruct((1,), jnp.int32),
        ),
        in_specs=[pl.BlockSpec(memory_space=pltpu.VMEM)] * 2,
        out_specs=(
            pl.BlockSpec(memory_space=pltpu.VMEM),
            pl.BlockSpec(memory_space=pltpu.SMEM),
        ),
        name="table",
    )(balance.reshape(1, BLOCKS), doc_block.reshape(1, BLOCKS))


def head_columns(head, width=HEAD_DIM):
    start = head * width
    return pl.ds(start if isinstance(start, int) else pl.multiple_of(start, width), width)


def softmax_mix(query, keys, values, above):
    scores = lax.dot_general(
        query, keys, (((1,), (1,)), ((), ())), preferred_element_type=jnp.float32
    )
    own = jnp.where(above, -jnp.inf, scores[:, :BLOCK])
    if keys.shape[0] > BLOCK:
        scores = jnp.concatenate([own, scores[:, BLOCK:]], axis=1)
    else:
        scores = own
    top = jnp.max(scores, axis=1, keepdims=True)
    weights = jnp.exp2((scores - top) * SCALE).astype(jnp.bfloat16)
    mixed = jnp.dot(weights, values, preferred_element_type=jnp.float32)
    return (mixed[:, :HEAD_DIM] / mixed[:, HEAD_DIM:]).astype(jnp.bfloat16)


def causal():
    return lax.broadcasted_iota(jnp.int32, (BLOCK, BLOCK), 1) > lax.broadcasted_iota(
        jnp.int32, (BLOCK, BLOCK), 0
    )


def with_ones(values):
    return jnp.concatenate([values, jnp.ones((BLOCK, HEAD_DIM), jnp.bfloat16)], axis=1)


def exchange_kernel(cap, table_ref, key_ref, value_ref, query_ref, last_ref, part_ref, *scratch):
    pieces, landed, held, packed, final = [
        scratch[k * CHUNKS : (k + 1) * CHUNKS] for k in range(5)
    ]
    rest = scratch[5 * CHUNKS :]
    windows = rest[: CHUNKS - 1] + (last_ref,)
    query, mixed = rest[CHUNKS - 1], rest[CHUNKS : 2 * CHUNKS - 1]
    sends, arrivals, local = rest[2 * CHUNKS - 1 :]
    seq = lax.axis_index("seq")
    z = lax.axis_index("head")
    width = mixed[0].shape[1]

    def plane_peer(step):
        step = step * 13 % SEQ
        y = (seq // 8 + step // 8) % 4
        x = (seq // 2 + step // 2) % 4
        core = (seq + step) % 2
        return y * 8 + x * 2 + core

    barrier = pltpu.get_barrier_semaphore()

    def greet_plane(step, carry):
        pl.semaphore_signal(barrier, inc=1, device_id=(plane_peer(step), z), device_id_type=MESH)
        return carry

    def greet_z(step, carry):
        pl.semaphore_signal(barrier, inc=1, device_id=(seq, (z + step) % ZS), device_id_type=MESH)
        return carry

    lax.fori_loop(1, SEQ, greet_plane, 0)
    lax.fori_loop(1, ZS, greet_z, 0)
    fetch = pltpu.make_async_copy(
        query_ref.at[:, pl.ds(0, (CHUNKS - 1) * width)], query, local.at[CHUNKS]
    )
    fetch.start()

    for chunk in range(CHUNKS):
        for kind, source in enumerate((key_ref, value_ref)):
            for h in range(HEADS):
                for tile in range(TILES):
                    for t in range(2):
                        row = t * BLOCK + tile * 16
                        pieces[chunk][(kind * HEADS + h) * TILES + tile, t] = source[
                            row : row + 16, head_columns(chunk * HEADS + h)
                        ]
    pl.semaphore_wait(barrier, SEQ - 1 + ZS - 1)

    def spread(chunk):
        def send(step, carry):
            peer = plane_peer(step)
            pltpu.make_async_remote_copy(
                src_ref=pieces[chunk].at[peer],
                dst_ref=landed[chunk].at[seq],
                send_sem=sends.at[0, chunk],
                recv_sem=arrivals.at[0, chunk],
                device_id=(peer, z),
                device_id_type=MESH,
            ).start()
            return carry

        lax.fori_loop(1, SEQ, send, 0)
        landed[chunk][seq] = pieces[chunk][seq]

    def across(chunk):
        whole = landed[chunk].at[pl.ds(0, SEQ - 1)]
        pltpu.make_async_copy(whole, whole, arrivals.at[0, chunk]).wait()

        def pack(step, carry):
            other = (z + step) % ZS
            for k in range(cap):
                index = table_ref[k, other]
                packed[chunk][other, k] = landed[chunk][index // 2, index % 2]
            pltpu.make_async_remote_copy(
                src_ref=packed[chunk].at[other],
                dst_ref=held[chunk].at[pl.ds(ITEMS + z * cap, cap)],
                send_sem=sends.at[1, chunk],
                recv_sem=arrivals.at[1, chunk],
                device_id=(seq, other),
                device_id_type=MESH,
            ).start()
            return carry

        lax.fori_loop(1, ZS, pack, 0)

    def keep(chunk):
        def own(k, carry):
            held[chunk][2 * k] = landed[chunk][k, 0]
            held[chunk][2 * k + 1] = landed[chunk][k, 1]
            return carry

        lax.fori_loop(0, SEQ, own, 0)

        def blank(k, carry):
            held[chunk][ITEMS + z * cap + k] = jnp.zeros((16, HEAD_DIM), jnp.bfloat16)
            return carry

        lax.fori_loop(0, cap, blank, 0)

    def deliver(chunk):
        whole = held[chunk].at[pl.ds(0, (ZS - 1) * cap)]
        pltpu.make_async_copy(whole, whole, arrivals.at[1, chunk]).wait()

        def fill(peer):
            for n in range(NEED):
                row, w = peer * 2 + n // WINDOW, n % WINDOW
                index = table_ref[row, 8 + w] + table_ref[row, 11 + w] * cap
                final[chunk][peer, n] = held[chunk][index]

        def pack(step, carry):
            peer = plane_peer(step)
            fill(peer)
            pltpu.make_async_remote_copy(
                src_ref=final[chunk].at[peer],
                dst_ref=windows[chunk].at[seq],
                send_sem=sends.at[2, chunk],
                recv_sem=arrivals.at[2, chunk],
                device_id=(peer, z),
                device_id_type=MESH,
            ).start()
            return carry

        lax.fori_loop(1, SEQ, pack, 0)
        fill(seq)
        pltpu.make_async_copy(
            final[chunk].at[seq], windows[chunk].at[seq], local.at[chunk]
        ).start()

    def arrive(chunk):
        pltpu.make_async_copy(
            final[chunk].at[seq], windows[chunk].at[seq], local.at[chunk]
        ).wait()
        whole = windows[chunk].at[pl.ds(0, SEQ - 1)]
        pltpu.make_async_copy(whole, whole, arrivals.at[2, chunk]).wait()

    above = causal()

    def store(chunk):
        return pltpu.make_async_copy(mixed[chunk], part_ref.at[chunk], local.at[CHUNKS + 1 + chunk])

    def attend_chunk(chunk):
        def unit(u, carry):
            t, h = u % 2, u // 2
            rows = pl.ds(pl.multiple_of(t * BLOCK, BLOCK), BLOCK)
            head = chunk * HEADS + h
            used = table_ref[0, 15 + t]
            keys = [key_ref[rows, head_columns(head)]]
            values = [with_ones(value_ref[rows, head_columns(head)])]
            first = jnp.broadcast_to(keys[0][0:1, :], (BLOCK, HEAD_DIM))
            for w in range(WINDOW):
                tiles = pl.ds(h * TILES, TILES)
                key = windows[chunk][tiles, t * WINDOW + w].reshape(BLOCK, HEAD_DIM)
                tiles = pl.ds((HEADS + h) * TILES, TILES)
                value = windows[chunk][tiles, t * WINDOW + w].reshape(BLOCK, HEAD_DIM)
                value = with_ones(value)
                keys.append(jnp.where(used > w, key, first))
                values.append(jnp.where(used > w, value, jnp.zeros_like(value)))
            keys = jnp.concatenate(keys, axis=0)
            values = jnp.concatenate(values, axis=0)
            for g in range(8):
                block = query[rows, head_columns(head * 8 + g)]
                mixed[chunk][rows, head_columns(h * 8 + g)] = softmax_mix(
                    block, keys, values, above
                )
            return carry

        lax.fori_loop(0, 2 * HEADS, unit, 0)
        store(chunk).start()

    spread(0)
    across(0)
    spread(1)
    keep(0)
    across(1)
    spread(2)
    keep(1)
    deliver(0)
    across(2)
    spread(3)
    keep(2)
    deliver(1)
    across(3)
    keep(3)
    fetch.wait()
    arrive(0)
    attend_chunk(0)
    deliver(2)
    arrive(1)
    attend_chunk(1)
    deliver(3)
    arrive(2)
    attend_chunk(2)
    arrive(3)
    for chunk in range(CHUNKS):
        gone = pieces[chunk].at[pl.ds(0, SEQ - 1)]
        pltpu.make_async_copy(gone, gone, sends.at[0, chunk]).wait()
        gone = packed[chunk].at[pl.ds(0, ZS - 1)]
        pltpu.make_async_copy(gone, gone, sends.at[1, chunk]).wait()
        gone = final[chunk].at[pl.ds(0, SEQ - 1)]
        pltpu.make_async_copy(gone, gone, sends.at[2, chunk]).wait()
    for chunk in range(CHUNKS - 1):
        store(chunk).wait()


def exchange(ident, table, keys, values, queries):
    cap = CAPS[ident]
    tokens, width = queries.shape[0], queries.shape[1] // CHUNKS
    bf16 = jnp.bfloat16
    tile = (16, HEAD_DIM)
    shapes = ((SEQ, 2), (SEQ, 2), (ITEMS + ZS * cap,), (ZS, cap), (SEQ, NEED))
    buffers = [pltpu.VMEM(s + tile, bf16) for s in shapes for _ in range(CHUNKS)]
    buffers += [pltpu.VMEM((SEQ, NEED) + tile, bf16)] * (CHUNKS - 1)
    buffers += [pltpu.VMEM((tokens, (CHUNKS - 1) * width), bf16)]
    buffers += [pltpu.VMEM((tokens, width), bf16)] * (CHUNKS - 1)
    return pl.pallas_call(
        functools.partial(exchange_kernel, cap),
        out_shape=(
            jax.ShapeDtypeStruct((SEQ, NEED) + tile, bf16),
            jax.ShapeDtypeStruct((CHUNKS - 1, tokens, width), bf16),
        ),
        in_specs=[
            pl.BlockSpec(memory_space=pltpu.SMEM),
            pl.BlockSpec(memory_space=pltpu.VMEM),
            pl.BlockSpec(memory_space=pltpu.VMEM),
            pl.BlockSpec(memory_space=pl.ANY),
        ],
        out_specs=(pl.BlockSpec(memory_space=pl.ANY), pl.BlockSpec(memory_space=pl.ANY)),
        scratch_shapes=buffers
        + [
            pltpu.SemaphoreType.DMA((3, CHUNKS)),
            pltpu.SemaphoreType.DMA((3, CHUNKS)),
            pltpu.SemaphoreType.DMA((2 * CHUNKS,)),
        ],
        compiler_params=pltpu.CompilerParams(
            collective_id=ident, has_side_effects=True, vmem_limit_bytes=48 * MIB
        ),
        name=f"exchange_{cap}",
    )(table, keys, values, queries)


def finish_kernel(
    table_ref, query_ref, key_ref, value_ref, window_ref, part_ref, out_ref, mixed, sems
):
    step = pl.program_id(0)
    width = query_ref.shape[1]
    part_width = part_ref.shape[2]
    above = causal()

    def parts():
        return [
            pltpu.make_async_copy(
                part_ref.at[c], out_ref.at[:, pl.ds(c * part_width, part_width)], sems.at[HEADS + c]
            )
            for c in range(CHUNKS - 1)
        ]

    def store(h):
        return pltpu.make_async_copy(
            mixed.at[h], out_ref.at[:, head_columns((CHUNKS - 1) * HEADS + h, width)], sems.at[h]
        )

    @pl.when(step == 0)
    def _():
        for copy in parts():
            copy.start()

    def block(t, windows):
        rows = slice(t * BLOCK, (t + 1) * BLOCK)
        keys = [key_ref[rows, :]]
        values = [with_ones(value_ref[rows, :])]
        for w in range(windows):
            n = t * WINDOW + w
            tiles = pl.ds(step * TILES, TILES)
            keys.append(window_ref[tiles, n].reshape(BLOCK, HEAD_DIM))
            tiles = pl.ds((HEADS + step) * TILES, TILES)
            values.append(with_ones(window_ref[tiles, n].reshape(BLOCK, HEAD_DIM)))
        keys = jnp.concatenate(keys, axis=0)
        values = jnp.concatenate(values, axis=0)
        for g in range(8):
            mixed[step, rows, head_columns(g)] = softmax_mix(
                query_ref[rows, head_columns(g)], keys, values, above
            )

    for t in range(2):
        for windows in range(WINDOW + 1):
            pl.when(table_ref[0, 15 + t] == windows)(functools.partial(block, t, windows))
    store(step).start()

    @pl.when(step == HEADS - 1)
    def _():
        for h in range(HEADS):
            store(h).wait()
        for copy in parts():
            copy.wait()


def finish(table, queries, keys, values, window, part):
    tokens = queries.shape[0]
    columns = queries.shape[1] // KV
    first = (CHUNKS - 1) * HEADS
    return pl.pallas_call(
        finish_kernel,
        out_shape=jax.ShapeDtypeStruct(queries.shape, queries.dtype),
        grid=(HEADS,),
        in_specs=[
            pl.BlockSpec(memory_space=pltpu.SMEM),
            pl.BlockSpec((tokens, columns), lambda k: (0, first + k)),
            pl.BlockSpec((tokens, HEAD_DIM), lambda k: (0, first + k)),
            pl.BlockSpec((tokens, HEAD_DIM), lambda k: (0, first + k)),
            pl.BlockSpec(window.shape, lambda k: (0, 0, 0, 0)),
            pl.BlockSpec(memory_space=pl.ANY),
        ],
        out_specs=pl.BlockSpec(memory_space=pl.ANY),
        scratch_shapes=[
            pltpu.VMEM((HEADS, tokens, columns), queries.dtype),
            pltpu.SemaphoreType.DMA((HEADS + CHUNKS - 1,)),
        ],
        compiler_params=pltpu.CompilerParams(vmem_limit_bytes=40 * MIB),
        name="finish",
    )(table, queries, keys, values, window, part)


def shards(queries, keys, values, doc_block, balance):
    table, branch = make_table(balance, doc_block)
    window, part = lax.switch(
        branch[0],
        [functools.partial(exchange, ident) for ident in range(len(CAPS))],
        table,
        keys,
        values,
        queries,
    )
    return finish(table, queries, keys, values, window, part)


def solution(mesh):
    in_specs = (
        P(("seq", "head"), None),
        P(("seq", "head"), None),
        P(("seq", "head"), None),
        P(),
        P(),
    )
    out_specs = P(("seq", "head"), None)
    return jax.shard_map(shards, mesh=mesh, in_specs=in_specs, out_specs=out_specs, check_vma=False)
```

```python
import functools
import math

import jax
import jax.numpy as jnp
from jax import lax
from jax.experimental import pallas as pl
from jax.experimental.pallas import tpu as pltpu
from jax.sharding import PartitionSpec as P

HEAD_DIM = 128
BLOCK = 128
BLOCKS = 512
GROUP = 16
KV = 8
SEQ = 32
ZS = 8
ITEMS = 64
WINDOW = 3
NEED = 2 * WINDOW
TILES = BLOCK // 16
CHIPS = SEQ // 2
CHUNK_HEADS = ((0,), (1, 2), (3, 4), (5, 6), (7,))
CHUNK_SIDE = (1, None, None, None, 0)
CHUNKS = len(CHUNK_HEADS)
LAST = CHUNKS - 1
PARTS = CHUNKS + 1
CAPS = (13, 14, 15, 17, 64)
MIB = 1024 * 1024
MESH = pl.DeviceIdType.MESH
SCALE = math.log2(math.e) / math.sqrt(HEAD_DIM)


def table_kernel(balance_ref, doc_ref, table_ref, branch_ref):
    seq = lax.axis_index("seq")
    z = lax.axis_index("head")
    f32 = jnp.float32
    balance = balance_ref[...]
    doc = doc_ref[...].astype(f32)
    rows = lax.broadcasted_iota(jnp.int32, (BLOCKS, BLOCKS), 0)
    cols = lax.broadcasted_iota(jnp.int32, (BLOCKS, BLOCKS), 1)
    doc_col = jnp.sum(jnp.where(rows == cols, doc, 0.0), axis=1, keepdims=True)
    label = jnp.sum(jnp.where(rows == balance, doc_col, 0.0), axis=0, keepdims=True)
    position = lax.broadcasted_iota(jnp.int32, (1, BLOCKS), 1)
    z_of = balance % GROUP // 2
    item = balance // GROUP * 2 + balance % 2
    zs = lax.broadcasted_iota(jnp.int32, (ZS, BLOCKS), 0)
    uses = (zs == z_of).astype(f32)
    wanted = jnp.zeros((ZS, BLOCKS), f32)
    valid = []
    for w in range(1, WINDOW + 1):
        same = (position % GROUP >= w) & (pltpu.roll(label, w, 1) == label)
        same = same.astype(f32)
        valid.append(same)
        wanted = jnp.maximum(wanted, pltpu.roll(uses * same, BLOCKS - w, 1))
    to_mine = jnp.sum(jnp.where(zs == z, wanted, 0.0), axis=0, keepdims=True)
    sends = jnp.where(z_of == z, wanted, 0.0)
    receives = uses * to_mine
    members = jnp.concatenate([sends, receives], axis=0)
    before = (rows < cols).astype(f32).astype(jnp.bfloat16)
    ranks = jnp.dot(members.astype(jnp.bfloat16), before, preferred_element_type=f32)
    counts = jnp.zeros((ZS, 1), f32)
    for other in range(ZS):
        count = jnp.sum(uses * wanted[other : other + 1, :], axis=1, keepdims=True)
        own = lax.broadcasted_iota(jnp.int32, (ZS, 1), 0) == other
        counts = jnp.maximum(counts, jnp.where(own, 0.0, count))
    most = jnp.max(counts)
    branch = jnp.int32(0)
    for cap in CAPS[:-1]:
        branch = branch + (most > cap).astype(jnp.int32)
    branch_ref[0] = branch
    rank_in = jnp.sum(receives * ranks[ZS:, :], axis=0, keepdims=True)
    item_float = item.astype(f32)
    lanes = lax.broadcasted_iota(jnp.int32, (ITEMS, 128), 1)
    table = jnp.zeros((ITEMS, 128), f32)
    slot = lax.broadcasted_iota(jnp.int32, (ITEMS, BLOCKS), 0)
    for other in range(ZS):
        rank = jnp.where(members[other : other + 1, :] > 0.0, ranks[other : other + 1, :], -1.0)
        picked = jnp.sum(
            jnp.where(slot.astype(f32) == rank, item_float, 0.0), axis=1, keepdims=True
        )
        table = jnp.where(lanes == other, picked, table)
    match = slot // 2 * GROUP + z * 2 + slot % 2 == balance
    place = jnp.where(z_of == z, item_float, ITEMS + rank_in)
    region = jnp.where(z_of == z, 0.0, z_of.astype(f32))
    for lane, what in ((8, place), (11, region)):
        for w in range(1, WINDOW + 1):
            source = pltpu.roll(what, w, 1) * valid[w - 1]
            found = jnp.sum(jnp.where(match, source, 0.0), axis=1, keepdims=True)
            table = jnp.where(lanes == lane + w - 1, found, table)
    in_use = valid[0] + valid[0] * valid[1] + valid[0] * valid[1] * valid[2]
    for t in range(2):
        mine = balance == seq * GROUP + z * 2 + t
        used = jnp.sum(jnp.where(mine, in_use, 0.0), axis=1, keepdims=True)
        table = jnp.where(lanes == 15 + t, used, table)
    table_ref[...] = table.astype(jnp.int32)


def make_table(balance, doc_block):
    return pl.pallas_call(
        table_kernel,
        out_shape=(
            jax.ShapeDtypeStruct((ITEMS, 128), jnp.int32),
            jax.ShapeDtypeStruct((1,), jnp.int32),
        ),
        in_specs=[pl.BlockSpec(memory_space=pltpu.VMEM)] * 2,
        out_specs=(
            pl.BlockSpec(memory_space=pltpu.VMEM),
            pl.BlockSpec(memory_space=pltpu.SMEM),
        ),
        name="table",
    )(balance.reshape(1, BLOCKS), doc_block.reshape(1, BLOCKS))


def head_columns(head, width=HEAD_DIM):
    start = head * width
    return pl.ds(start if isinstance(start, int) else pl.multiple_of(start, width), width)


def softmax_mix(query, keys, values, above):
    scores = lax.dot_general(
        query, keys, (((1,), (1,)), ((), ())), preferred_element_type=jnp.float32
    )
    own = jnp.where(above, -jnp.inf, scores[:, :BLOCK])
    if keys.shape[0] > BLOCK:
        scores = jnp.concatenate([own, scores[:, BLOCK:]], axis=1)
    else:
        scores = own
    top = jnp.max(scores, axis=1, keepdims=True)
    weights = jnp.exp2((scores - top) * SCALE).astype(jnp.bfloat16)
    mixed = jnp.dot(weights, values, preferred_element_type=jnp.float32)
    return (mixed[:, :HEAD_DIM] / mixed[:, HEAD_DIM:]).astype(jnp.bfloat16)


def causal():
    return lax.broadcasted_iota(jnp.int32, (BLOCK, BLOCK), 1) > lax.broadcasted_iota(
        jnp.int32, (BLOCK, BLOCK), 0
    )


def with_ones(values):
    return jnp.concatenate([values, jnp.ones((BLOCK, HEAD_DIM), jnp.bfloat16)], axis=1)


def exchange_kernel(cap, table_ref, key_ref, value_ref, query_ref, out_ref, *scratch):
    pieces, landed, held, packed = [scratch[k * CHUNKS : (k + 1) * CHUNKS] for k in range(4)]
    rest = scratch[4 * CHUNKS :]
    final, windows = rest[:PARTS], rest[PARTS : 2 * PARTS]
    query, mixed, sends, arrivals, deliveries, local = rest[2 * PARTS :]
    seq = lax.axis_index("seq")
    z = lax.axis_index("head")
    core = seq % 2
    chip = seq // 2
    width = query.shape[1] // KV

    def plane_peer(step):
        step = step * 5 % SEQ
        y = (seq // 8 + step // 8) % 4
        x = (seq // 2 + step // 2) % 4
        core = (seq + step) % 2
        return y * 8 + x * 2 + core

    def chip_peer(step):
        step = step * 5 % CHIPS
        return (chip // 4 + step // 4) % 4 * 4 + (chip + step) % 4

    barrier = pltpu.get_barrier_semaphore()

    def greet_plane(step, carry):
        pl.semaphore_signal(barrier, inc=1, device_id=(plane_peer(step), z), device_id_type=MESH)
        return carry

    def greet_z(step, carry):
        pl.semaphore_signal(barrier, inc=1, device_id=(seq, (z + step) % ZS), device_id_type=MESH)
        return carry

    lax.fori_loop(1, SEQ, greet_plane, 0)
    lax.fori_loop(1, ZS, greet_z, 0)
    fetch = pltpu.make_async_copy(query_ref, query, local.at[PARTS])
    fetch.start()

    for chunk, heads in enumerate(CHUNK_HEADS):
        for kind, source in enumerate((key_ref, value_ref)):
            for h, head in enumerate(heads):
                for tile in range(TILES):
                    for t in range(2):
                        row = t * BLOCK + tile * 16
                        pieces[chunk][(kind * len(heads) + h) * TILES + tile, t] = source[
                            row : row + 16, head_columns(head)
                        ]
    pl.semaphore_wait(barrier, SEQ - 1 + ZS - 1)

    def spread(chunk):
        side = CHUNK_SIDE[chunk]

        def send(piece, peer):
            pltpu.make_async_remote_copy(
                src_ref=pieces[chunk].at[piece],
                dst_ref=landed[chunk].at[seq],
                send_sem=sends.at[0, chunk],
                recv_sem=arrivals.at[0, chunk],
                device_id=(peer, z),
                device_id_type=MESH,
            ).start()

        def to_device(step, carry):
            peer = plane_peer(step)
            send(peer, peer)
            return carry

        def to_chip(step, carry):
            peer = chip_peer(step)
            send(peer, peer * 2 + side)
            return carry

        if side is None:
            lax.fori_loop(1, SEQ, to_device, 0)
            landed[chunk][seq] = pieces[chunk][seq]
            return
        lax.fori_loop(1, CHIPS, to_chip, 0)

        @pl.when(core == side)
        def _():
            landed[chunk][seq] = pieces[chunk][chip]

        @pl.when(core != side)
        def _():
            send(chip, chip * 2 + side)

    def across(chunk):
        whole = landed[chunk].at[pl.ds(0, SEQ - 1)]
        pltpu.make_async_copy(whole, whole, arrivals.at[0, chunk]).wait()

        def pack(step, carry):
            other = (z + step) % ZS
            for k in range(cap):
                index = table_ref[k, other]
                packed[chunk][other, k] = landed[chunk][index // 2, index % 2]
            pltpu.make_async_remote_copy(
                src_ref=packed[chunk].at[other],
                dst_ref=held[chunk].at[pl.ds(ITEMS + z * cap, cap)],
                send_sem=sends.at[1, chunk],
                recv_sem=arrivals.at[1, chunk],
                device_id=(seq, other),
                device_id_type=MESH,
            ).start()
            return carry

        lax.fori_loop(1, ZS, pack, 0)

    def keep(chunk):
        def own(k, carry):
            held[chunk][2 * k] = landed[chunk][k, 0]
            held[chunk][2 * k + 1] = landed[chunk][k, 1]
            return carry

        lax.fori_loop(0, SEQ, own, 0)

        def blank(k, carry):
            held[chunk][ITEMS + z * cap + k] = jnp.zeros((16, HEAD_DIM), jnp.bfloat16)
            return carry

        lax.fori_loop(0, cap, blank, 0)

    def part_slots(part):
        if part < LAST:
            return part, 0, NEED
        return LAST, (part - LAST) * WINDOW, WINDOW

    def collect(chunk):
        whole = held[chunk].at[pl.ds(0, (ZS - 1) * cap)]
        pltpu.make_async_copy(whole, whole, arrivals.at[1, chunk]).wait()

    def source_of(part):
        return seq if CHUNK_SIDE[part_slots(part)[0]] is None else chip

    def own_part(part):
        return pltpu.make_async_copy(
            final[part].at[seq], windows[part].at[source_of(part)], local.at[part]
        )

    def deliver(part):
        chunk, first, count = part_slots(part)

        def fill(peer):
            for k in range(count):
                n = first + k
                row, w = peer * 2 + n // WINDOW, n % WINDOW
                index = table_ref[row, 8 + w] + table_ref[row, 11 + w] * cap
                final[part][peer, k] = held[chunk][index]

        def pack(step, carry):
            peer = plane_peer(step)
            fill(peer)
            pltpu.make_async_remote_copy(
                src_ref=final[part].at[peer],
                dst_ref=windows[part].at[source_of(part)],
                send_sem=deliveries.at[0, part],
                recv_sem=deliveries.at[1, part],
                device_id=(peer, z),
                device_id_type=MESH,
            ).start()
            return carry

        lax.fori_loop(1, SEQ, pack, 0)
        fill(seq)
        own_part(part).start()

    def arrive(part):
        side = CHUNK_SIDE[part_slots(part)[0]]

        def take(count):
            whole = windows[part].at[pl.ds(0, count)]
            pltpu.make_async_copy(whole, whole, deliveries.at[1, part]).wait()

        def take_own():
            own_part(part).wait()
            take((SEQ if side is None else CHIPS) - 1)

        if side is None:
            take_own()
            return
        pl.when(core == side)(take_own)
        pl.when(core != side)(functools.partial(take, CHIPS))

    above = causal()

    def store(part):
        chunk, first, count = part_slots(part)
        rows = pl.ds(first // WINDOW * BLOCK, count // WINDOW * BLOCK)
        heads = CHUNK_HEADS[chunk]
        columns = pl.ds(heads[0] * width, len(heads) * width)
        return pltpu.make_async_copy(
            mixed.at[rows, columns],
            out_ref.at[rows, columns],
            local.at[PARTS + 1 + part],
        )

    def attend(part):
        chunk, first, count = part_slots(part)
        blocks = count // WINDOW
        heads = CHUNK_HEADS[chunk]

        def unit(u, carry):
            k, h = u % blocks, u // blocks
            t = k + first // WINDOW
            rows = pl.ds(pl.multiple_of(t * BLOCK, BLOCK), BLOCK)
            head = heads[0] + h
            used = table_ref[0, 15 + t]
            keys = [key_ref[rows, head_columns(head)]]
            values = [with_ones(value_ref[rows, head_columns(head)])]
            start = jnp.broadcast_to(keys[0][0:1, :], (BLOCK, HEAD_DIM))
            for w in range(WINDOW):
                tiles = pl.ds(h * TILES, TILES)
                key = windows[part][tiles, k * WINDOW + w].reshape(BLOCK, HEAD_DIM)
                tiles = pl.ds((len(heads) + h) * TILES, TILES)
                value = windows[part][tiles, k * WINDOW + w].reshape(BLOCK, HEAD_DIM)
                value = with_ones(value)
                keys.append(jnp.where(used > w, key, start))
                values.append(jnp.where(used > w, value, jnp.zeros_like(value)))
            keys = jnp.concatenate(keys, axis=0)
            values = jnp.concatenate(values, axis=0)
            for g in range(8):
                block = query[rows, head_columns(head * 8 + g)]
                mixed[rows, head_columns(head * 8 + g)] = softmax_mix(
                    block, keys, values, above
                )
            return carry

        lax.fori_loop(0, blocks * len(heads), unit, 0)
        store(part).start()

    def handler(what, part):
        pl.when(core == CHUNK_SIDE[min(part, LAST)])(functools.partial(what, part))

    spread(0)
    spread(1)
    handler(across, 0)
    across(1)
    spread(2)
    across(2)
    spread(3)
    handler(keep, 0)
    keep(1)
    handler(collect, 0)
    handler(deliver, 0)
    keep(2)
    across(3)
    spread(4)
    keep(3)
    collect(1)
    deliver(1)
    handler(across, 4)
    handler(keep, 4)
    fetch.wait()
    arrive(0)
    attend(0)
    collect(2)
    deliver(2)
    arrive(1)
    attend(1)
    collect(3)
    deliver(3)
    arrive(2)
    handler(collect, 4)
    handler(deliver, 4)
    handler(deliver, 5)
    attend(2)
    arrive(3)
    attend(3)
    arrive(4)
    attend(4)
    arrive(5)
    attend(5)

    def gone(ref, count, sem):
        whole = ref.at[pl.ds(0, count)]
        pltpu.make_async_copy(whole, whole, sem).wait()

    def drain(chunk):
        gone(packed[chunk], ZS - 1, sends.at[1, chunk])
        for part in range(PARTS):
            if part_slots(part)[0] == chunk:
                gone(final[part], SEQ - 1, deliveries.at[0, part])

    for chunk, side in enumerate(CHUNK_SIDE):
        if side is None:
            gone(pieces[chunk], SEQ - 1, sends.at[0, chunk])
            drain(chunk)
            continue
        for own, count in ((side, CHIPS - 1), (1 - side, CHIPS)):
            pl.when(core == own)(
                functools.partial(gone, pieces[chunk], count, sends.at[0, chunk])
            )
        handler(drain, chunk)
    for part in range(PARTS):
        store(part).wait()


def exchange(ident, table, keys, values, queries):
    cap = CAPS[ident]
    bf16 = jnp.bfloat16
    tile = (16, HEAD_DIM)

    def vmem(*shape):
        return pltpu.VMEM(shape + tile, bf16)

    buffers = [vmem(len(heads) * CHIPS, 2) for heads in CHUNK_HEADS]
    for shape in ((SEQ, 2), (ITEMS + ZS * cap,), (ZS, cap)):
        buffers += [vmem(*shape)] * CHUNKS
    buffers += [vmem(SEQ, NEED)] * LAST + [vmem(SEQ, WINDOW)] * 2
    buffers += [vmem(len(heads) * CHIPS, NEED) for heads in CHUNK_HEADS[:LAST]]
    buffers += [vmem(len(CHUNK_HEADS[LAST]) * CHIPS, WINDOW)] * 2
    buffers += [pltpu.VMEM(queries.shape, bf16)] * 2
    return pl.pallas_call(
        functools.partial(exchange_kernel, cap),
        out_shape=jax.ShapeDtypeStruct(queries.shape, queries.dtype),
        in_specs=[
            pl.BlockSpec(memory_space=pltpu.SMEM),
            pl.BlockSpec(memory_space=pltpu.VMEM),
            pl.BlockSpec(memory_space=pltpu.VMEM),
            pl.BlockSpec(memory_space=pl.ANY),
        ],
        out_specs=pl.BlockSpec(memory_space=pl.ANY),
        scratch_shapes=buffers
        + [
            pltpu.SemaphoreType.DMA((2, CHUNKS)),
            pltpu.SemaphoreType.DMA((2, CHUNKS)),
            pltpu.SemaphoreType.DMA((2, PARTS)),
            pltpu.SemaphoreType.DMA((2 * PARTS + 1,)),
        ],
        compiler_params=pltpu.CompilerParams(
            collective_id=ident, has_side_effects=True, vmem_limit_bytes=44 * MIB
        ),
        name=f"exchange_{cap}",
    )(table, keys, values, queries)


def shards(queries, keys, values, doc_block, balance):
    table, branch = make_table(balance, doc_block)
    return lax.switch(
        branch[0],
        [functools.partial(exchange, ident) for ident in range(len(CAPS))],
        table,
        keys,
        values,
        queries,
    )


def solution(mesh):
    in_specs = (
        P(("seq", "head"), None),
        P(("seq", "head"), None),
        P(("seq", "head"), None),
        P(),
        P(),
    )
    out_specs = P(("seq", "head"), None)
    return jax.shard_map(shards, mesh=mesh, in_specs=in_specs, out_specs=out_specs, check_vma=False)
```

```python
import functools
import math

import jax
import jax.numpy as jnp
from jax import lax
from jax.experimental import pallas as pl
from jax.experimental.pallas import tpu as pltpu
from jax.sharding import PartitionSpec as P

HEAD_DIM = 128
BLOCK = 128
BLOCKS = 512
GROUP = 16
KV = 8
SEQ = 32
ZS = 8
ITEMS = 64
WINDOW = 3
NEED = 2 * WINDOW
CHUNKS = 4
HEADS = KV // CHUNKS
TILES = BLOCK // 16
CAPS = (15, 17, 64)
MIB = 1024 * 1024
MESH = pl.DeviceIdType.MESH
SCALE = math.log2(math.e) / math.sqrt(HEAD_DIM)


def table_kernel(balance_ref, doc_ref, table_ref, branch_ref):
    seq = lax.axis_index("seq")
    z = lax.axis_index("head")
    f32 = jnp.float32
    balance = balance_ref[...]
    doc = doc_ref[...].astype(f32)
    rows = lax.broadcasted_iota(jnp.int32, (BLOCKS, BLOCKS), 0)
    cols = lax.broadcasted_iota(jnp.int32, (BLOCKS, BLOCKS), 1)
    doc_col = jnp.sum(jnp.where(rows == cols, doc, 0.0), axis=1, keepdims=True)
    label = jnp.sum(jnp.where(rows == balance, doc_col, 0.0), axis=0, keepdims=True)
    position = lax.broadcasted_iota(jnp.int32, (1, BLOCKS), 1)
    z_of = balance % GROUP // 2
    item = balance // GROUP * 2 + balance % 2
    zs = lax.broadcasted_iota(jnp.int32, (ZS, BLOCKS), 0)
    uses = (zs == z_of).astype(f32)
    wanted = jnp.zeros((ZS, BLOCKS), f32)
    valid = []
    for w in range(1, WINDOW + 1):
        same = (position % GROUP >= w) & (pltpu.roll(label, w, 1) == label)
        same = same.astype(f32)
        valid.append(same)
        wanted = jnp.maximum(wanted, pltpu.roll(uses * same, BLOCKS - w, 1))
    to_mine = jnp.sum(jnp.where(zs == z, wanted, 0.0), axis=0, keepdims=True)
    sends = jnp.where(z_of == z, wanted, 0.0)
    receives = uses * to_mine
    members = jnp.concatenate([sends, receives], axis=0)
    before = (rows < cols).astype(f32).astype(jnp.bfloat16)
    ranks = jnp.dot(members.astype(jnp.bfloat16), before, preferred_element_type=f32)
    counts = jnp.zeros((ZS, 1), f32)
    for other in range(ZS):
        count = jnp.sum(uses * wanted[other : other + 1, :], axis=1, keepdims=True)
        own = lax.broadcasted_iota(jnp.int32, (ZS, 1), 0) == other
        counts = jnp.maximum(counts, jnp.where(own, 0.0, count))
    most = jnp.max(counts)
    branch = jnp.int32(0)
    for cap in CAPS[:-1]:
        branch = branch + (most > cap).astype(jnp.int32)
    branch_ref[0] = branch
    rank_in = jnp.sum(receives * ranks[ZS:, :], axis=0, keepdims=True)
    item_float = item.astype(f32)
    lanes = lax.broadcasted_iota(jnp.int32, (ITEMS, 128), 1)
    table = jnp.zeros((ITEMS, 128), f32)
    slot = lax.broadcasted_iota(jnp.int32, (ITEMS, BLOCKS), 0)
    for other in range(ZS):
        rank = jnp.where(members[other : other + 1, :] > 0.0, ranks[other : other + 1, :], -1.0)
        picked = jnp.sum(
            jnp.where(slot.astype(f32) == rank, item_float, 0.0), axis=1, keepdims=True
        )
        table = jnp.where(lanes == other, picked, table)
    match = slot // 2 * GROUP + z * 2 + slot % 2 == balance
    place = jnp.where(z_of == z, item_float, ITEMS + rank_in)
    region = jnp.where(z_of == z, 0.0, z_of.astype(f32))
    for lane, what in ((8, place), (11, region)):
        for w in range(1, WINDOW + 1):
            source = pltpu.roll(what, w, 1) * valid[w - 1]
            found = jnp.sum(jnp.where(match, source, 0.0), axis=1, keepdims=True)
            table = jnp.where(lanes == lane + w - 1, found, table)
    in_use = valid[0] + valid[0] * valid[1] + valid[0] * valid[1] * valid[2]
    for t in range(2):
        mine = balance == seq * GROUP + z * 2 + t
        used = jnp.sum(jnp.where(mine, in_use, 0.0), axis=1, keepdims=True)
        table = jnp.where(lanes == 15 + t, used, table)
    table_ref[...] = table.astype(jnp.int32)


def make_table(balance, doc_block):
    return pl.pallas_call(
        table_kernel,
        out_shape=(
            jax.ShapeDtypeStruct((ITEMS, 128), jnp.int32),
            jax.ShapeDtypeStruct((1,), jnp.int32),
        ),
        in_specs=[pl.BlockSpec(memory_space=pltpu.VMEM)] * 2,
        out_specs=(
            pl.BlockSpec(memory_space=pltpu.VMEM),
            pl.BlockSpec(memory_space=pltpu.SMEM),
        ),
        name="table",
    )(balance.reshape(1, BLOCKS), doc_block.reshape(1, BLOCKS))


def head_columns(head, width=HEAD_DIM):
    start = head * width
    return pl.ds(start if isinstance(start, int) else pl.multiple_of(start, width), width)


def softmax_mix(query, keys, values, above):
    scores = lax.dot_general(
        query, keys, (((1,), (1,)), ((), ())), preferred_element_type=jnp.float32
    )
    own = jnp.where(above, -jnp.inf, scores[:, :BLOCK])
    if keys.shape[0] > BLOCK:
        scores = jnp.concatenate([own, scores[:, BLOCK:]], axis=1)
    else:
        scores = own
    top = jnp.max(scores, axis=1, keepdims=True)
    weights = jnp.exp2((scores - top) * SCALE).astype(jnp.bfloat16)
    mixed = jnp.dot(weights, values, preferred_element_type=jnp.float32)
    return (mixed[:, :HEAD_DIM] / mixed[:, HEAD_DIM:]).astype(jnp.bfloat16)


def causal():
    return lax.broadcasted_iota(jnp.int32, (BLOCK, BLOCK), 1) > lax.broadcasted_iota(
        jnp.int32, (BLOCK, BLOCK), 0
    )


def with_ones(values):
    return jnp.concatenate([values, jnp.ones((BLOCK, HEAD_DIM), jnp.bfloat16)], axis=1)


def exchange_kernel(cap, table_ref, key_ref, value_ref, query_ref, out_ref, *scratch):
    pieces, landed, held, packed = [scratch[k * CHUNKS : (k + 1) * CHUNKS] for k in range(4)]
    rest = scratch[4 * CHUNKS :]
    final, windows = rest[: CHUNKS + 1], rest[CHUNKS + 1 : 2 * CHUNKS + 2]
    query, mixed, sends, arrivals, deliveries, local = rest[2 * CHUNKS + 2 :]
    seq = lax.axis_index("seq")
    z = lax.axis_index("head")
    width = mixed.shape[2]

    def plane_peer(step):
        step = step * 5 % SEQ
        y = (seq // 8 + step // 8) % 4
        x = (seq // 2 + step // 2) % 4
        core = (seq + step) % 2
        return y * 8 + x * 2 + core

    barrier = pltpu.get_barrier_semaphore()

    def greet_plane(step, carry):
        pl.semaphore_signal(barrier, inc=1, device_id=(plane_peer(step), z), device_id_type=MESH)
        return carry

    def greet_z(step, carry):
        pl.semaphore_signal(barrier, inc=1, device_id=(seq, (z + step) % ZS), device_id_type=MESH)
        return carry

    lax.fori_loop(1, SEQ, greet_plane, 0)
    lax.fori_loop(1, ZS, greet_z, 0)
    fetch = pltpu.make_async_copy(query_ref, query, local.at[CHUNKS + 1])
    fetch.start()

    for chunk in range(CHUNKS):
        for kind, source in enumerate((key_ref, value_ref)):
            for h in range(HEADS):
                for tile in range(TILES):
                    for t in range(2):
                        row = t * BLOCK + tile * 16
                        pieces[chunk][(kind * HEADS + h) * TILES + tile, t] = source[
                            row : row + 16, head_columns(chunk * HEADS + h)
                        ]
    pl.semaphore_wait(barrier, SEQ - 1 + ZS - 1)

    def spread(chunk):
        def send(step, carry):
            peer = plane_peer(step)
            pltpu.make_async_remote_copy(
                src_ref=pieces[chunk].at[peer],
                dst_ref=landed[chunk].at[seq],
                send_sem=sends.at[0, chunk],
                recv_sem=arrivals.at[0, chunk],
                device_id=(peer, z),
                device_id_type=MESH,
            ).start()
            return carry

        lax.fori_loop(1, SEQ, send, 0)
        landed[chunk][seq] = pieces[chunk][seq]

    def across(chunk):
        whole = landed[chunk].at[pl.ds(0, SEQ - 1)]
        pltpu.make_async_copy(whole, whole, arrivals.at[0, chunk]).wait()

        def pack(step, carry):
            other = (z + step) % ZS
            for k in range(cap):
                index = table_ref[k, other]
                packed[chunk][other, k] = landed[chunk][index // 2, index % 2]
            pltpu.make_async_remote_copy(
                src_ref=packed[chunk].at[other],
                dst_ref=held[chunk].at[pl.ds(ITEMS + z * cap, cap)],
                send_sem=sends.at[1, chunk],
                recv_sem=arrivals.at[1, chunk],
                device_id=(seq, other),
                device_id_type=MESH,
            ).start()
            return carry

        lax.fori_loop(1, ZS, pack, 0)

    def keep(chunk):
        def own(k, carry):
            held[chunk][2 * k] = landed[chunk][k, 0]
            held[chunk][2 * k + 1] = landed[chunk][k, 1]
            return carry

        lax.fori_loop(0, SEQ, own, 0)

        def blank(k, carry):
            held[chunk][ITEMS + z * cap + k] = jnp.zeros((16, HEAD_DIM), jnp.bfloat16)
            return carry

        lax.fori_loop(0, cap, blank, 0)

    def part_slots(part):
        if part < CHUNKS - 1:
            return part, 0, NEED
        return CHUNKS - 1, (part - CHUNKS + 1) * WINDOW, WINDOW

    def collect(chunk):
        whole = held[chunk].at[pl.ds(0, (ZS - 1) * cap)]
        pltpu.make_async_copy(whole, whole, arrivals.at[1, chunk]).wait()

    def own_part(part):
        return pltpu.make_async_copy(final[part].at[seq], windows[part].at[seq], local.at[part])

    def deliver(part):
        chunk, first, count = part_slots(part)

        def fill(peer):
            for k in range(count):
                n = first + k
                row, w = peer * 2 + n // WINDOW, n % WINDOW
                index = table_ref[row, 8 + w] + table_ref[row, 11 + w] * cap
                final[part][peer, k] = held[chunk][index]

        def pack(step, carry):
            peer = plane_peer(step)
            fill(peer)
            pltpu.make_async_remote_copy(
                src_ref=final[part].at[peer],
                dst_ref=windows[part].at[seq],
                send_sem=deliveries.at[0, part],
                recv_sem=deliveries.at[1, part],
                device_id=(peer, z),
                device_id_type=MESH,
            ).start()
            return carry

        lax.fori_loop(1, SEQ, pack, 0)
        fill(seq)
        own_part(part).start()

    def arrive(part):
        own_part(part).wait()
        whole = windows[part].at[pl.ds(0, SEQ - 1)]
        pltpu.make_async_copy(whole, whole, deliveries.at[1, part]).wait()

    above = causal()

    def store(part):
        chunk, first, count = part_slots(part)
        rows = pl.ds(0 if count == NEED else first // WINDOW * BLOCK, count // WINDOW * BLOCK)
        return pltpu.make_async_copy(
            mixed.at[chunk, rows],
            out_ref.at[rows, pl.ds(chunk * width, width)],
            local.at[CHUNKS + 2 + part],
        )

    def attend(part):
        chunk, first, count = part_slots(part)
        blocks = count // WINDOW

        def unit(u, carry):
            k, h = u % blocks, u // blocks
            t = k + first // WINDOW
            rows = pl.ds(pl.multiple_of(t * BLOCK, BLOCK), BLOCK)
            head = chunk * HEADS + h
            used = table_ref[0, 15 + t]
            keys = [key_ref[rows, head_columns(head)]]
            values = [with_ones(value_ref[rows, head_columns(head)])]
            start = jnp.broadcast_to(keys[0][0:1, :], (BLOCK, HEAD_DIM))
            for w in range(WINDOW):
                tiles = pl.ds(h * TILES, TILES)
                key = windows[part][tiles, k * WINDOW + w].reshape(BLOCK, HEAD_DIM)
                tiles = pl.ds((HEADS + h) * TILES, TILES)
                value = windows[part][tiles, k * WINDOW + w].reshape(BLOCK, HEAD_DIM)
                value = with_ones(value)
                keys.append(jnp.where(used > w, key, start))
                values.append(jnp.where(used > w, value, jnp.zeros_like(value)))
            keys = jnp.concatenate(keys, axis=0)
            values = jnp.concatenate(values, axis=0)
            for g in range(8):
                block = query[rows, head_columns(head * 8 + g)]
                mixed[chunk, rows, head_columns(h * 8 + g)] = softmax_mix(
                    block, keys, values, above
                )
            return carry

        lax.fori_loop(0, blocks * HEADS, unit, 0)
        store(part).start()

    spread(0)
    across(0)
    spread(1)
    keep(0)
    across(1)
    spread(2)
    keep(1)
    collect(0)
    deliver(0)
    across(2)
    spread(3)
    keep(2)
    collect(1)
    deliver(1)
    across(3)
    keep(3)
    fetch.wait()
    arrive(0)
    attend(0)
    collect(2)
    deliver(2)
    arrive(1)
    attend(1)
    collect(3)
    deliver(3)
    deliver(4)
    arrive(2)
    attend(2)
    arrive(3)
    attend(3)
    arrive(4)
    attend(4)
    for chunk in range(CHUNKS):
        gone = pieces[chunk].at[pl.ds(0, SEQ - 1)]
        pltpu.make_async_copy(gone, gone, sends.at[0, chunk]).wait()
        gone = packed[chunk].at[pl.ds(0, ZS - 1)]
        pltpu.make_async_copy(gone, gone, sends.at[1, chunk]).wait()
    for part in range(CHUNKS + 1):
        gone = final[part].at[pl.ds(0, SEQ - 1)]
        pltpu.make_async_copy(gone, gone, deliveries.at[0, part]).wait()
        store(part).wait()


def exchange(ident, table, keys, values, queries):
    cap = CAPS[ident]
    tokens, width = queries.shape[0], queries.shape[1] // CHUNKS
    bf16 = jnp.bfloat16
    tile = (16, HEAD_DIM)
    shapes = ((SEQ, 2), (SEQ, 2), (ITEMS + ZS * cap,), (ZS, cap))
    buffers = [pltpu.VMEM(s + tile, bf16) for s in shapes for _ in range(CHUNKS)]
    parts = [pltpu.VMEM((SEQ, NEED) + tile, bf16)] * (CHUNKS - 1)
    parts += [pltpu.VMEM((SEQ, WINDOW) + tile, bf16)] * 2
    buffers += parts + parts
    buffers += [
        pltpu.VMEM((tokens, CHUNKS * width), bf16),
        pltpu.VMEM((CHUNKS, tokens, width), bf16),
    ]
    return pl.pallas_call(
        functools.partial(exchange_kernel, cap),
        out_shape=jax.ShapeDtypeStruct(queries.shape, queries.dtype),
        in_specs=[
            pl.BlockSpec(memory_space=pltpu.SMEM),
            pl.BlockSpec(memory_space=pltpu.VMEM),
            pl.BlockSpec(memory_space=pltpu.VMEM),
            pl.BlockSpec(memory_space=pl.ANY),
        ],
        out_specs=pl.BlockSpec(memory_space=pl.ANY),
        scratch_shapes=buffers
        + [
            pltpu.SemaphoreType.DMA((2, CHUNKS)),
            pltpu.SemaphoreType.DMA((2, CHUNKS)),
            pltpu.SemaphoreType.DMA((2, CHUNKS + 1)),
            pltpu.SemaphoreType.DMA((2 * CHUNKS + 3,)),
        ],
        compiler_params=pltpu.CompilerParams(
            collective_id=ident, has_side_effects=True, vmem_limit_bytes=44 * MIB
        ),
        name=f"exchange_{cap}",
    )(table, keys, values, queries)


def shards(queries, keys, values, doc_block, balance):
    table, branch = make_table(balance, doc_block)
    return lax.switch(
        branch[0],
        [functools.partial(exchange, ident) for ident in range(len(CAPS))],
        table,
        keys,
        values,
        queries,
    )


def solution(mesh):
    in_specs = (
        P(("seq", "head"), None),
        P(("seq", "head"), None),
        P(("seq", "head"), None),
        P(),
        P(),
    )
    out_specs = P(("seq", "head"), None)
    return jax.shard_map(shards, mesh=mesh, in_specs=in_specs, out_specs=out_specs, check_vma=False)
```
